32 devices in a mesh: row: 4 (over z), col: 4 (over x, core), dep: 2 (over y).
Axes of the slice: x: 2, y: 2, z: 4, core: 2. Of those that a mesh axis runs over, the one named last changes fastest.
Arguments:
- tokens: bfloat16 [512, 8192], P(('dep', 'col'), 'row'), may hold values from -6 to 6
- gate_weight: bfloat16 [8192, 14336], P('row', 'col'), may hold values from -0.0625 to 0.0625
- up_weight: bfloat16 [8192, 14336], P('row', 'col'), may hold values from -0.0625 to 0.0625
- cotangent: bfloat16 [512, 14336], P(('dep', 'row'), 'col'), may hold values from -6 to 6
Outputs:
- hidden: bfloat16 [512, 14336], P(('dep', 'row'), 'col')
- grad_tokens: bfloat16 [512, 8192], P(('dep', 'col'), 'row')
- grad_gate_weight: bfloat16 [8192, 14336], P('row', ('col', 'dep'))
- grad_up_weight: bfloat16 [8192, 14336], P('row', ('col', 'dep'))
The draws below stay inside these ranges and needn't reach their ends.
All inputs are finite; a program needn't handle non-finite values.
Results may differ from the reference program's by a relative error of at most 0.02.
Values may be sent and summed in bfloat16 or wider, within the bound.
A program may use at most 128 MiB of HBM per device.

```python
import jax
import jax.numpy as jnp
from jax import lax

D = 8192
FF = 14336
SLICE = 256
TOKENS = 512
N_ROW = 4
N_COL = 4
N_DEP = 2


def level_of(key, dims, cuts, least, largest):
    level, own = 1.0, jax.random.fold_in(key, 6)
    for axis_at, parts in cuts:
        steps = jnp.exp(jax.random.uniform(jax.random.fold_in(own, axis_at), (parts,), jnp.float32, least / len(cuts), largest / len(cuts)))
        level = level * jnp.repeat(steps, dims[axis_at] // parts).reshape([-1 if axis == axis_at else 1 for axis in range(len(dims))])
    return level


def bell_draw(stream_key, dims, width, reach, cuts=(), kind=jnp.bfloat16):
    factor_of = level_of(stream_key, dims, cuts, -0.22, 0.18) if cuts else 1.0
    array = jax.random.normal(stream_key, dims, jnp.float32) * width * factor_of
    return jnp.minimum(jnp.maximum(array, -reach), reach).astype(kind)


def setup_inputs(seed: int = 0) -> dict:
    arg_keys = jax.random.split(jax.random.key(seed), 5)
    return {
        "tokens": bell_draw(arg_keys[0], (TOKENS, D), 1.0, 6.0, ((0, 8), (1, 4))),
        "gate_weight": bell_draw(arg_keys[1], (D, FF), D ** -0.5, 0.0625, ((0, 4), (1, 4))),
        "up_weight": bell_draw(arg_keys[2], (D, FF), D ** -0.5, 0.0625, ((0, 4), (1, 4))),
        "cotangent": bell_draw(arg_keys[3], (TOKENS, FF), 1.0, 6.0, ((0, 8), (1, 4))),
    }


def rounded(value):
    return lax.optimization_barrier(value.astype(jnp.bfloat16)).astype(jnp.float32)


def reference(tokens, gate_weight, up_weight, cotangent):
    feat_block = D // N_ROW
    gate = jnp.zeros((TOKENS, FF), jnp.float32)
    up = jnp.zeros((TOKENS, FF), jnp.float32)
    for index in range(N_ROW):
        lower = index * feat_block
        rows = tokens[:, lower:lower + feat_block]
        gate = gate + rounded(jnp.dot(rows, gate_weight[lower:lower + feat_block], preferred_element_type=jnp.float32))
        up = up + rounded(jnp.dot(rows, up_weight[lower:lower + feat_block], preferred_element_type=jnp.float32))
    sigma = jax.nn.sigmoid(gate)
    active = gate * sigma
    hidden = (active * up).astype(jnp.bfloat16)
    upstream = cotangent.astype(jnp.float32)
    grad_gate = (upstream * up * sigma * (1.0 + gate * (1.0 - sigma))).astype(jnp.bfloat16)
    grad_up = (upstream * active).astype(jnp.bfloat16)
    hid_block = FF // N_COL
    grad_tokens = jnp.zeros((TOKENS, D), jnp.float32)
    for index in range(N_COL):
        lower = index * hid_block
        term = jnp.dot(grad_gate[:, lower:lower + hid_block], gate_weight[:, lower:lower + hid_block].T, preferred_element_type=jnp.float32)
        term = term + jnp.dot(grad_up[:, lower:lower + hid_block], up_weight[:, lower:lower + hid_block].T, preferred_element_type=jnp.float32)
        grad_tokens = grad_tokens + rounded(term)
    sum_gate = jnp.zeros((D, FF), jnp.float32)
    sum_up = jnp.zeros((D, FF), jnp.float32)
    for index in range(N_DEP):
        lower = index * SLICE
        rows = tokens[lower:lower + SLICE].T
        sum_gate = sum_gate + rounded(jnp.dot(rows, grad_gate[lower:lower + SLICE], preferred_element_type=jnp.float32))
        sum_up = sum_up + rounded(jnp.dot(rows, grad_up[lower:lower + SLICE], preferred_element_type=jnp.float32))
    return hidden, grad_tokens.astype(jnp.bfloat16), sum_gate.astype(jnp.bfloat16), sum_up.astype(jnp.bfloat16)
```

```python
import jax
import jax.numpy as jnp
from jax import lax
from jax.sharding import PartitionSpec as P


def swapped(block, n_dep):
    parts = [block]
    for _ in range(n_dep - 1):
        parts.append(lax.ppermute(parts[-1], "dep", [(i, (i + 1) % n_dep) for i in range(n_dep)]))
    return parts


def on_device(n_dep, tokens, gate_weight, up_weight, cotangent):
    width = gate_weight.shape[1]
    share = width // n_dep
    me = lax.axis_index("dep")
    gathered = lax.all_gather(tokens, "col", axis=0, tiled=True)
    all_tokens = jnp.concatenate(swapped(gathered, n_dep), axis=0)

    def dot(a, b):
        return jnp.dot(a, b, preferred_element_type=jnp.float32)

    def scattered(part):
        return lax.psum_scatter(
            part.astype(jnp.bfloat16), "row", scatter_dimension=0, tiled=True
        ).astype(jnp.float32)

    gate = scattered(dot(gathered, gate_weight))
    up = scattered(dot(gathered, up_weight))
    sigma = jax.nn.sigmoid(gate)
    active = gate * sigma
    hidden = (active * up).astype(jnp.bfloat16)
    upstream = cotangent.astype(jnp.float32)
    grad_gate = (upstream * up * sigma * (1.0 + gate * (1.0 - sigma))).astype(jnp.bfloat16)
    grad_up = (upstream * active).astype(jnp.bfloat16)
    full_up = lax.all_gather(grad_up, "row", axis=0, tiled=True)
    full_gate = lax.all_gather(grad_gate, "row", axis=0, tiled=True)

    def exchanged(full):
        parts = [lax.dynamic_slice_in_dim(full, me * share, share, 1)]
        for step in range(1, n_dep):
            to = lax.rem(me + step, n_dep)
            block = lax.dynamic_slice_in_dim(full, to * share, share, 1)
            parts.append(lax.ppermute(block, "dep", [(i, (i + step) % n_dep) for i in range(n_dep)]))
        return jnp.concatenate(parts, axis=0)

    transposed = (((1,), (1,)), ((), ()))
    contract = (((0,), (0,)), ((), ()))
    all_up = exchanged(full_up)
    all_gate = exchanged(full_gate)
    term = lax.dot_general(full_up, up_weight, transposed, preferred_element_type=jnp.float32)
    term = term + lax.dot_general(full_gate, gate_weight, transposed, preferred_element_type=jnp.float32)
    grad_tokens = lax.psum_scatter(
        term.astype(jnp.bfloat16), "col", scatter_dimension=0, tiled=True
    )
    sum_up = lax.dot_general(all_tokens, all_up, contract, preferred_element_type=jnp.float32)
    sum_gate = lax.dot_general(all_tokens, all_gate, contract, preferred_element_type=jnp.float32)
    return (hidden, grad_tokens, sum_gate.astype(jnp.bfloat16), sum_up.astype(jnp.bfloat16))


def solution(mesh):
    n_dep = mesh.shape["dep"]
    return jax.shard_map(
        lambda *args: on_device(n_dep, *args),
        mesh=mesh,
        in_specs=(
            P(("dep", "col"), "row"),
            P("row", "col"),
            P("row", "col"),
            P(("dep", "row"), "col"),
        ),
        out_specs=(
            P(("dep", "row"), "col"),
            P(("dep", "col"), "row"),
            P("row", ("col", "dep")),
            P("row", ("col", "dep")),
        ),
        check_vma=False,
    )
```

```python
import functools

import jax
import jax.numpy as jnp
from jax import lax
from jax.experimental import pallas as pl
from jax.experimental.pallas import tpu as pltpu
from jax.sharding import PartitionSpec as P

MESH = pl.DeviceIdType.MESH
WIDTH = 128


def kernel(
    n_row, n_col, n_dep, w,
    tokens_ref, gate_w_ref, up_w_ref, cot_ref,
    hidden_ref, part_ref, all_tok_ref, all_gate_ref, all_up_ref,
    tok, weights, own, from_left, from_right, grads, acc,
    w_sem, tok_send, tok_recv, tok_local, slice_send, slice_recv,
    rs_send, left_recv, right_recv, ag_right_send, ag_left_send, ag_recv,
    dep_send, dep_recv, dep_local,
):
    me = lax.axis_index("row")
    my_col = lax.axis_index("col")
    my_dep = lax.axis_index("dep")
    chunks = weights.shape[0]
    depth = weights.shape[1]
    lanes = weights.shape[2]
    share = all_gate_ref.shape[3]
    last = n_row - 1
    out_refs = (all_gate_ref, all_up_ref)
    tokens_n = tok.shape[0] * tok.shape[1]

    def weight_copy(c, h, k):
        ref = (gate_w_ref, up_w_ref)[k]
        at = pl.multiple_of(h * share + c * w, w)
        return pltpu.make_async_copy(
            ref.at[:, pl.ds(at, w)],
            weights.at[c, :, pl.ds((h * 2 + k) * w, w)],
            w_sem.at[c, h * 2 + k],
        )

    def load_weights(c):
        for h in range(n_dep):
            for k in range(2):
                weight_copy(c, h, k).start()

    @pl.loop(0, chunks)
    def _(c):
        load_weights(c)

    barrier = pltpu.get_barrier_semaphore()
    for step in range(1, n_col):
        pl.semaphore_signal(barrier, inc=1, device_id={"col": lax.rem(my_col + step, n_col)}, device_id_type=MESH)
    for step in range(1, n_dep):
        pl.semaphore_signal(barrier, inc=1, device_id={"dep": lax.rem(my_dep + step, n_dep)}, device_id_type=MESH)

    @pl.when(me > 0)
    def _():
        pl.semaphore_signal(barrier, inc=1, device_id={"row": me - 1}, device_id_type=MESH)

    @pl.when(me < last)
    def _():
        pl.semaphore_signal(barrier, inc=1, device_id={"row": me + 1}, device_id_type=MESH)

    peers = n_col - 1 + n_dep - 1
    inside = jnp.logical_and(me > 0, me < last)

    @pl.when(inside)
    def _():
        pl.semaphore_wait(barrier, peers + 2)

    @pl.when(jnp.logical_not(inside))
    def _():
        pl.semaphore_wait(barrier, peers + 1)

    def token_copy(step):
        return pltpu.make_async_remote_copy(
            src_ref=tokens_ref, dst_ref=tok.at[my_col],
            send_sem=tok_send.at[step], recv_sem=tok_recv.at[step],
            device_id={"col": lax.rem(my_col + step, n_col)}, device_id_type=MESH,
        )

    for step in range(1, n_col):
        token_copy(step).start()
    tok[pl.ds(my_col, 1)] = tokens_ref[...][None]
    acc[...] = jnp.zeros_like(acc)
    for step in range(1, n_col):
        token_copy(step).wait_recv()

    def slice_copy(step):
        return pltpu.make_async_remote_copy(
            src_ref=tok, dst_ref=all_tok_ref.at[my_dep],
            send_sem=slice_send.at[step], recv_sem=slice_recv.at[step],
            device_id={"dep": lax.rem(my_dep + step, n_dep)}, device_id_type=MESH,
        )

    tok_out = pltpu.make_async_copy(tok, all_tok_ref.at[my_dep], tok_local)
    for step in range(1, n_dep):
        slice_copy(step).start()
    tok_out.start()

    def rs_right(c, j):
        return pltpu.make_async_remote_copy(
            src_ref=own.at[c, j], dst_ref=from_left.at[c, j],
            send_sem=rs_send.at[c, j], recv_sem=left_recv.at[c, j],
            device_id={"row": me + 1}, device_id_type=MESH,
        )

    def rs_left(c, j):
        return pltpu.make_async_remote_copy(
            src_ref=own.at[c, j], dst_ref=from_right.at[c, j],
            send_sem=rs_send.at[c, j], recv_sem=right_recv.at[c, j],
            device_id={"row": me - 1}, device_id_type=MESH,
        )

    def ag_right(c, j):
        return pltpu.make_async_remote_copy(
            src_ref=grads.at[c, j], dst_ref=grads.at[c, j],
            send_sem=ag_right_send.at[c, j], recv_sem=ag_recv.at[c, j],
            device_id={"row": me + 1}, device_id_type=MESH,
        )

    def ag_left(c, j):
        return pltpu.make_async_remote_copy(
            src_ref=grads.at[c, j], dst_ref=grads.at[c, j],
            send_sem=ag_left_send.at[c, j], recv_sem=ag_recv.at[c, j],
            device_id={"row": me - 1}, device_id_type=MESH,
        )

    def dep_copy(c, step, k):
        to = lax.rem(my_dep + step, n_dep)
        return pltpu.make_async_remote_copy(
            src_ref=grads.at[c, :, :, pl.ds(pl.multiple_of((to * 2 + k) * w, w), w)],
            dst_ref=out_refs[k].at[my_dep, :, :, pl.ds(pl.multiple_of(c * w, w), w)],
            send_sem=dep_send.at[c, step, k], recv_sem=dep_recv.at[c, step, k],
            device_id={"dep": to}, device_id_type=MESH,
        )

    def dep_own(c, k):
        return pltpu.make_async_copy(
            grads.at[c, :, :, pl.ds(pl.multiple_of((my_dep * 2 + k) * w, w), w)],
            out_refs[k].at[my_dep, :, :, pl.ds(pl.multiple_of(c * w, w), w)],
            dep_local.at[c, k],
        )

    def valid(c):
        return jnp.logical_and(c >= 0, c < chunks)

    def forward(c):
        for h in range(n_dep):
            for k in range(2):
                weight_copy(c, h, k).wait()
        lhs = tok[...].reshape(tokens_n, depth)
        for at in range(0, lanes, 256):
            own[c, :, :, at:at + 256] = (
                jnp.dot(lhs, weights[c, :, at:at + 256], preferred_element_type=jnp.float32)
                .astype(jnp.bfloat16)
                .reshape(n_row, tokens_n // n_row, 256)
            )

    def added(ref, other):
        ref[...] = (ref[...].astype(jnp.float32) + other[...].astype(jnp.float32)).astype(jnp.bfloat16)

    def reduce_right(c):
        for j in range(1, n_row):
            @pl.when(j > me)
            def _():
                @pl.when(me > 0)
                def _():
                    rs_right(c, j).wait_recv()
                    added(own.at[c, j], from_left.at[c, j])
                rs_right(c, j).start()

    def reduce_left(c):
        for j in range(n_row - 1):
            @pl.when(j < me)
            def _():
                @pl.when(me < last)
                def _():
                    rs_left(c, j).wait_recv()
                    added(own.at[c, j], from_right.at[c, j])
                rs_left(c, j).start()

    def finish(c):
        @pl.when(me > 0)
        def _():
            rs_right(c, me).wait_recv()

        @pl.when(me < last)
        def _():
            rs_left(c, me).wait_recv()

        for h in range(n_dep):
            at = h * 2 * w

            def total(lo):
                piece = pl.ds(lo, w)
                value = own[c, me, :, piece].astype(jnp.float32)
                value = value + jnp.where(me > 0, from_left[c, me, :, piece].astype(jnp.float32), 0.0)
                return value + jnp.where(me < last, from_right[c, me, :, piece].astype(jnp.float32), 0.0)

            gate, up = total(at), total(at + w)
            sigma = 1.0 / (1.0 + jnp.exp(-gate))
            active = gate * sigma
            columns = pl.ds(pl.multiple_of(h * share + c * w, w), w)
            hidden_ref[:, columns] = (active * up).astype(jnp.bfloat16)
            upstream = cot_ref[:, columns].astype(jnp.float32)
            grads[c, me, :, pl.ds(at, w)] = (
                upstream * up * sigma * (1.0 + gate * (1.0 - sigma))
            ).astype(jnp.bfloat16)
            grads[c, me, :, pl.ds(at + w, w)] = (upstream * active).astype(jnp.bfloat16)

        @pl.when(me < last)
        def _():
            ag_right(c, me).start()

        @pl.when(me > 0)
        def _():
            ag_left(c, me).start()

    def relay(t):
        for away in range(1, n_row):
            c = t - last - away

            @pl.when(valid(c))
            def _():
                @pl.when(me - away >= 0)
                def _():
                    ag_right(c, me - away).wait_recv()

                    @pl.when(me < last)
                    def _():
                        ag_right(c, me - away).start()

                @pl.when(me + away <= last)
                def _():
                    ag_left(c, me + away).wait_recv()

                    @pl.when(me > 0)
                    def _():
                        ag_left(c, me + away).start()

    def backward(c):
        for step in range(1, n_dep):
            for k in range(2):
                dep_copy(c, step, k).start()
        for k in range(2):
            dep_own(c, k).start()
        lhs = grads[c].reshape(tokens_n, lanes)
        tile = min(512, depth)

        @pl.loop(0, depth // tile)
        def _(i):
            rows = pl.ds(pl.multiple_of(i * tile, tile), tile)
            acc[:, rows] += lax.dot_general(
                lhs, weights[c, rows, :], (((1,), (1,)), ((), ())), preferred_element_type=jnp.float32
            )

    @pl.loop(0, chunks + 2 * last)
    def _(t):
        @pl.when(t < chunks)
        def _():
            forward(t)

        c_right = t - me
        @pl.when(valid(c_right))
        def _():
            reduce_right(c_right)

        c_left = t - (last - me)
        @pl.when(valid(c_left))
        def _():
            reduce_left(c_left)

        relay(t)

        c_own = t - last
        @pl.when(valid(c_own))
        def _():
            finish(c_own)

        c_back = t - last - jnp.maximum(me, last - me)
        @pl.when(valid(c_back))
        def _():
            backward(c_back)

    part_ref[...] = acc[...].astype(jnp.bfloat16)

    for step in range(1, n_col):
        token_copy(step).wait_send()
    for step in range(1, n_dep):
        slice_copy(step).wait()
    tok_out.wait()

    @pl.loop(0, chunks)
    def _(c):
        for j in range(n_row):
            @pl.when(j > me)
            def _():
                rs_right(c, j).wait_send()

            @pl.when(j < me)
            def _():
                rs_left(c, j).wait_send()

            @pl.when(jnp.logical_and(j <= me, me < last))
            def _():
                ag_right(c, j).wait_send()

            @pl.when(jnp.logical_and(j >= me, me > 0))
            def _():
                ag_left(c, j).wait_send()
        for k in range(2):
            for step in range(1, n_dep):
                dep_copy(c, step, k).wait()
            dep_own(c, k).wait()


def exchange(n_row, n_col, n_dep, tokens, gate_weight, up_weight, cotangent):
    rows, depth = tokens.shape
    width = gate_weight.shape[1]
    share = width // n_dep
    w = WIDTH
    chunks = share // w
    lanes = 2 * n_dep * w
    tokens_n = rows * n_col
    block = tokens_n // n_row
    bf16 = jnp.bfloat16
    vmem, hbm = pl.BlockSpec(memory_space=pltpu.VMEM), pl.BlockSpec(memory_space=pl.ANY)
    dma = pltpu.SemaphoreType.DMA
    return pl.pallas_call(
        functools.partial(kernel, n_row, n_col, n_dep, w),
        out_shape=(
            jax.ShapeDtypeStruct((block, width), bf16),
            jax.ShapeDtypeStruct((tokens_n, depth), bf16),
            jax.ShapeDtypeStruct((n_dep, n_col, rows, depth), bf16),
            jax.ShapeDtypeStruct((n_dep, n_row, block, share), bf16),
            jax.ShapeDtypeStruct((n_dep, n_row, block, share), bf16),
        ),
        in_specs=[vmem, hbm, hbm, vmem],
        out_specs=(vmem, vmem, hbm, hbm, hbm),
        scratch_shapes=[
            pltpu.VMEM((n_col, rows, depth), bf16),
            pltpu.VMEM((chunks, depth, lanes), bf16),
            pltpu.VMEM((chunks, n_row, block, lanes), bf16),
            pltpu.VMEM((chunks, n_row, block, lanes), bf16),
            pltpu.VMEM((chunks, n_row, block, lanes), bf16),
            pltpu.VMEM((chunks, n_row, block, lanes), bf16),
            pltpu.VMEM((tokens_n, depth), jnp.float32),
            dma((chunks, 2 * n_dep)),
            dma((n_col,)), dma((n_col,)), dma,
            dma((n_dep,)), dma((n_dep,)),
            dma((chunks, n_row)), dma((chunks, n_row)), dma((chunks, n_row)),
            dma((chunks, n_row)), dma((chunks, n_row)), dma((chunks, n_row)),
            dma((chunks, n_dep, 2)), dma((chunks, n_dep, 2)), dma((chunks, 2)),
        ],
        compiler_params=pltpu.CompilerParams(
            collective_id=0, has_side_effects=True, vmem_limit_bytes=60 * 1024 * 1024
        ),
        cost_estimate=pl.CostEstimate(
            flops=8 * tokens_n * depth * width,
            bytes_accessed=4 * depth * width,
            transcendentals=block * width,
        ),
    )(tokens, gate_weight, up_weight, cotangent)


def on_device(n_row, n_col, n_dep, tokens, gate_weight, up_weight, cotangent):
    depth = tokens.shape[1]
    hidden, part, all_tokens, all_gate, all_up = exchange(
        n_row, n_col, n_dep, tokens, gate_weight, up_weight, cotangent
    )
    grad_tokens = lax.psum_scatter(part, "col", scatter_dimension=0, tiled=True)
    share = all_gate.shape[3]
    contract = (((0,), (0,)), ((), ()))
    flat = all_tokens.reshape(-1, depth)
    sums = [
        lax.dot_general(
            flat, grad.reshape(-1, share), contract, preferred_element_type=jnp.float32
        ).astype(jnp.bfloat16)
        for grad in (all_gate, all_up)
    ]
    return (hidden, grad_tokens, *sums)


def solution(mesh):
    sizes = tuple(mesh.shape[axis] for axis in ("row", "col", "dep"))
    return jax.shard_map(
        functools.partial(on_device, *sizes),
        mesh=mesh,
        in_specs=(
            P(("dep", "col"), "row"),
            P("row", "col"),
            P("row", "col"),
            P(("dep", "row"), "col"),
        ),
        out_specs=(
            P(("dep", "row"), "col"),
            P(("dep", "col"), "row"),
            P("row", ("col", "dep")),
            P("row", ("col", "dep")),
        ),
        check_vma=False,
    )
```

```python
import functools

import jax
import jax.numpy as jnp
from jax import lax
from jax.experimental import pallas as pl
from jax.experimental.pallas import tpu as pltpu
from jax.sharding import PartitionSpec as P

MESH = pl.DeviceIdType.MESH
WIDTH = 128
AHEAD = 2
SUM_LAG = 1
GATHER_LAG = 1


def kernel(
    n_row, n_col, n_dep, w,
    tokens_ref, gate_w_ref, up_w_ref, cot_ref,
    hidden_ref, part_ref, all_tok_ref, all_gate_ref, all_up_ref,
    tok, weights, own, from_left, from_right, grads, acc,
    w_sem, tok_send, tok_recv, tok_local, slice_send, slice_recv,
    rs_send, left_recv, right_recv, ag_right_send, ag_left_send, ag_recv,
    dep_send, dep_recv, dep_local,
):
    me = lax.axis_index("row")
    my_col = lax.axis_index("col")
    my_dep = lax.axis_index("dep")
    chunks = weights.shape[0]
    depth = weights.shape[1]
    lanes = weights.shape[2]
    share = all_gate_ref.shape[3]
    last = n_row - 1
    out_refs = (all_gate_ref, all_up_ref)
    tokens_n = tok.shape[0] * tok.shape[1]

    def weight_copy(c, h, k):
        ref = (gate_w_ref, up_w_ref)[k]
        at = pl.multiple_of(h * share + c * w, w)
        return pltpu.make_async_copy(
            ref.at[:, pl.ds(at, w)],
            weights.at[c, :, pl.ds((h * 2 + k) * w, w)],
            w_sem.at[c, h * 2 + k],
        )

    def load_weights(c):
        for h in range(n_dep):
            for k in range(2):
                weight_copy(c, h, k).start()

    @pl.loop(0, chunks)
    def _(c):
        load_weights(c)

    barrier = pltpu.get_barrier_semaphore()
    for step in range(1, n_col):
        pl.semaphore_signal(barrier, inc=1, device_id={"col": lax.rem(my_col + step, n_col)}, device_id_type=MESH)
    for step in range(1, n_dep):
        pl.semaphore_signal(barrier, inc=1, device_id={"dep": lax.rem(my_dep + step, n_dep)}, device_id_type=MESH)

    @pl.when(me > 0)
    def _():
        pl.semaphore_signal(barrier, inc=1, device_id={"row": me - 1}, device_id_type=MESH)

    @pl.when(me < last)
    def _():
        pl.semaphore_signal(barrier, inc=1, device_id={"row": me + 1}, device_id_type=MESH)

    peers = n_col - 1 + n_dep - 1
    inside = jnp.logical_and(me > 0, me < last)

    @pl.when(inside)
    def _():
        pl.semaphore_wait(barrier, peers + 2)

    @pl.when(jnp.logical_not(inside))
    def _():
        pl.semaphore_wait(barrier, peers + 1)

    other = my_col + 1 - 2 * lax.rem(my_col, 2)

    def token_copy(step):
        return pltpu.make_async_remote_copy(
            src_ref=tokens_ref, dst_ref=tok.at[my_col],
            send_sem=tok_send.at[step], recv_sem=tok_recv.at[step],
            device_id={"col": lax.rem(my_col + step, n_col)}, device_id_type=MESH,
        )

    def pair_copy(step):
        if step == 0:
            src, at = tokens_ref, my_col
        else:
            at = lax.rem(my_col - step + n_col, n_col)
            src = tok.at[at]
        return pltpu.make_async_remote_copy(
            src_ref=src, dst_ref=tok.at[at],
            send_sem=tok_send.at[step + 1], recv_sem=tok_recv.at[step + 1],
            device_id={"col": other}, device_id_type=MESH,
        )

    for step in range(2, n_col, 2):
        token_copy(step).start()
    pair_copy(0).start()
    tok[pl.ds(my_col, 1)] = tokens_ref[...][None]
    acc[...] = jnp.zeros_like(acc)
    for step in range(2, n_col, 2):
        token_copy(step).wait_recv()
        pair_copy(step).start()
    for step in range(0, n_col, 2):
        pair_copy(step).wait_recv()

    def slice_copy(step):
        return pltpu.make_async_remote_copy(
            src_ref=tok, dst_ref=all_tok_ref.at[my_dep],
            send_sem=slice_send.at[step], recv_sem=slice_recv.at[step],
            device_id={"dep": lax.rem(my_dep + step, n_dep)}, device_id_type=MESH,
        )

    tok_out = pltpu.make_async_copy(tok, all_tok_ref.at[my_dep], tok_local)
    for step in range(1, n_dep):
        slice_copy(step).start()
    tok_out.start()

    def rs_right(c, j):
        return pltpu.make_async_remote_copy(
            src_ref=own.at[c, j], dst_ref=from_left.at[c, j],
            send_sem=rs_send.at[c, j], recv_sem=left_recv.at[c, j],
            device_id={"row": me + 1}, device_id_type=MESH,
        )

    def rs_left(c, j):
        return pltpu.make_async_remote_copy(
            src_ref=own.at[c, j], dst_ref=from_right.at[c, j],
            send_sem=rs_send.at[c, j], recv_sem=right_recv.at[c, j],
            device_id={"row": me - 1}, device_id_type=MESH,
        )

    def ag_right(c, j):
        return pltpu.make_async_remote_copy(
            src_ref=grads.at[c, j], dst_ref=grads.at[c, j],
            send_sem=ag_right_send.at[c, j], recv_sem=ag_recv.at[c, j],
            device_id={"row": me + 1}, device_id_type=MESH,
        )

    def ag_left(c, j):
        return pltpu.make_async_remote_copy(
            src_ref=grads.at[c, j], dst_ref=grads.at[c, j],
            send_sem=ag_left_send.at[c, j], recv_sem=ag_recv.at[c, j],
            device_id={"row": me - 1}, device_id_type=MESH,
        )

    def dep_copy(c, step, k):
        to = lax.rem(my_dep + step, n_dep)
        return pltpu.make_async_remote_copy(
            src_ref=grads.at[c, :, :, pl.ds(pl.multiple_of((to * 2 + k) * w, w), w)],
            dst_ref=out_refs[k].at[my_dep, :, :, pl.ds(pl.multiple_of(c * w, w), w)],
            send_sem=dep_send.at[c, step, k], recv_sem=dep_recv.at[c, step, k],
            device_id={"dep": to}, device_id_type=MESH,
        )

    def dep_own(c, k):
        return pltpu.make_async_copy(
            grads.at[c, :, :, pl.ds(pl.multiple_of((my_dep * 2 + k) * w, w), w)],
            out_refs[k].at[my_dep, :, :, pl.ds(pl.multiple_of(c * w, w), w)],
            dep_local.at[c, k],
        )

    def ready(j):
        return (jnp.maximum(j, last - j) - 1) * SUM_LAG

    def valid(c):
        return jnp.logical_and(c >= 0, c < chunks)

    def forward(c):
        for h in range(n_dep):
            for k in range(2):
                weight_copy(c, h, k).wait()
        lhs = tok[...].reshape(tokens_n, depth)
        for at in range(0, lanes, 256):
            own[c, :, :, at:at + 256] = (
                jnp.dot(lhs, weights[c, :, at:at + 256], preferred_element_type=jnp.float32)
                .astype(jnp.bfloat16)
                .reshape(n_row, tokens_n // n_row, 256)
            )

    def added(ref, other):
        ref[...] = (ref[...].astype(jnp.float32) + other[...].astype(jnp.float32)).astype(jnp.bfloat16)

    def reduce_right(c):
        for j in reversed(range(1, n_row)):
            @pl.when(j > me)
            def _():
                @pl.when(me > 0)
                def _():
                    rs_right(c, j).wait_recv()
                    added(own.at[c, j], from_left.at[c, j])
                rs_right(c, j).start()

    def reduce_left(c):
        for j in range(n_row - 1):
            @pl.when(j < me)
            def _():
                @pl.when(me < last)
                def _():
                    rs_left(c, j).wait_recv()
                    added(own.at[c, j], from_right.at[c, j])
                rs_left(c, j).start()

    def finish(c):
        @pl.when(me > 0)
        def _():
            rs_right(c, me).wait_recv()

        @pl.when(me < last)
        def _():
            rs_left(c, me).wait_recv()

        for h in range(n_dep):
            at = h * 2 * w

            def total(lo):
                piece = pl.ds(lo, w)
                value = own[c, me, :, piece].astype(jnp.float32)
                value = value + jnp.where(me > 0, from_left[c, me, :, piece].astype(jnp.float32), 0.0)
                return value + jnp.where(me < last, from_right[c, me, :, piece].astype(jnp.float32), 0.0)

            gate, up = total(at), total(at + w)
            sigma = 1.0 / (1.0 + jnp.exp(-gate))
            active = gate * sigma
            columns = pl.ds(pl.multiple_of(h * share + c * w, w), w)
            hidden_ref[:, columns] = (active * up).astype(jnp.bfloat16)
            upstream = cot_ref[:, columns].astype(jnp.float32)
            grads[c, me, :, pl.ds(at, w)] = (
                upstream * up * sigma * (1.0 + gate * (1.0 - sigma))
            ).astype(jnp.bfloat16)
            grads[c, me, :, pl.ds(at + w, w)] = (upstream * active).astype(jnp.bfloat16)

        @pl.when(me < last)
        def _():
            ag_right(c, me).start()

        @pl.when(me > 0)
        def _():
            ag_left(c, me).start()

    def relay(t):
        for away in range(1, n_row):
            c_up = t - ready(me - away) - away * GATHER_LAG
            c_down = t - ready(me + away) - away * GATHER_LAG

            @pl.when(valid(c_up))
            def _():
                c = c_up

                @pl.when(me - away >= 0)
                def _():
                    ag_right(c, me - away).wait_recv()

                    @pl.when(me < last)
                    def _():
                        ag_right(c, me - away).start()

            @pl.when(valid(c_down))
            def _():
                c = c_down

                @pl.when(me + away <= last)
                def _():
                    ag_left(c, me + away).wait_recv()

                    @pl.when(me > 0)
                    def _():
                        ag_left(c, me + away).start()

    def backward(c):
        for step in range(1, n_dep):
            for k in range(2):
                dep_copy(c, step, k).start()
        for k in range(2):
            dep_own(c, k).start()
        lhs = grads[c].reshape(tokens_n, lanes)
        tile = min(512, depth)

        @pl.loop(0, depth // tile)
        def _(i):
            rows = pl.ds(pl.multiple_of(i * tile, tile), tile)
            acc[:, rows] += lax.dot_general(
                lhs, weights[c, rows, :], (((1,), (1,)), ((), ())), preferred_element_type=jnp.float32
            )

    def retire(c):
        for j in range(n_row):
            @pl.when(j > me)
            def _():
                rs_right(c, j).wait_send()

            @pl.when(j < me)
            def _():
                rs_left(c, j).wait_send()

            @pl.when(jnp.logical_and(j <= me, me < last))
            def _():
                ag_right(c, j).wait_send()

            @pl.when(jnp.logical_and(j >= me, me > 0))
            def _():
                ag_left(c, j).wait_send()
        for k in range(2):
            for step in range(1, n_dep):
                dep_copy(c, step, k).wait()
            dep_own(c, k).wait()

    def start(c):
        forward(c)

        @pl.when(me == 0)
        def _():
            reduce_right(c)

        @pl.when(me == last)
        def _():
            reduce_left(c)

    @pl.loop(0, AHEAD)
    def _(c):
        start(c)

    length = (last - 1) * SUM_LAG + last * GATHER_LAG
    done = 0
    for j in range(n_row):
        at = (max(j, last - j) - 1) * SUM_LAG
        done = jnp.maximum(done, at + jnp.abs(me - j) * GATHER_LAG)

    @pl.loop(0, chunks + length)
    def _(t):
        @pl.when(t + AHEAD < chunks)
        def _():
            start(t + AHEAD)

        c_right = t - (me - 1) * SUM_LAG
        @pl.when(jnp.logical_and(valid(c_right), me > 0))
        def _():
            reduce_right(c_right)

        c_left = t - (last - me - 1) * SUM_LAG
        @pl.when(jnp.logical_and(valid(c_left), me < last))
        def _():
            reduce_left(c_left)

        c_own = t - ready(me)
        @pl.when(valid(c_own))
        def _():
            finish(c_own)

        relay(t)

        c_back = t - done
        @pl.when(valid(c_back))
        def _():
            backward(c_back)

        c_out = t - length - 1
        @pl.when(valid(c_out))
        def _():
            retire(c_out)

    part_ref[...] = acc[...].astype(jnp.bfloat16)
    retire(chunks - 1)

    for step in range(2, n_col, 2):
        token_copy(step).wait_send()
    for step in range(0, n_col, 2):
        pair_copy(step).wait_send()
    for step in range(1, n_dep):
        slice_copy(step).wait()
    tok_out.wait()


def exchange(n_row, n_col, n_dep, tokens, gate_weight, up_weight, cotangent):
    rows, depth = tokens.shape
    width = gate_weight.shape[1]
    share = width // n_dep
    w = WIDTH
    chunks = share // w
    lanes = 2 * n_dep * w
    tokens_n = rows * n_col
    block = tokens_n // n_row
    bf16 = jnp.bfloat16
    vmem, hbm = pl.BlockSpec(memory_space=pltpu.VMEM), pl.BlockSpec(memory_space=pl.ANY)
    dma = pltpu.SemaphoreType.DMA
    return pl.pallas_call(
        functools.partial(kernel, n_row, n_col, n_dep, w),
        out_shape=(
            jax.ShapeDtypeStruct((block, width), bf16),
            jax.ShapeDtypeStruct((tokens_n, depth), bf16),
            jax.ShapeDtypeStruct((n_dep, n_col, rows, depth), bf16),
            jax.ShapeDtypeStruct((n_dep, n_row, block, share), bf16),
            jax.ShapeDtypeStruct((n_dep, n_row, block, share), bf16),
        ),
        in_specs=[vmem, hbm, hbm, vmem],
        out_specs=(vmem, vmem, hbm, hbm, hbm),
        scratch_shapes=[
            pltpu.VMEM((n_col, rows, depth), bf16),
            pltpu.VMEM((chunks, depth, lanes), bf16),
            pltpu.VMEM((chunks, n_row, block, lanes), bf16),
            pltpu.VMEM((chunks, n_row, block, lanes), bf16),
            pltpu.VMEM((chunks, n_row, block, lanes), bf16),
            pltpu.VMEM((chunks, n_row, block, lanes), bf16),
            pltpu.VMEM((tokens_n, depth), jnp.float32),
            dma((chunks, 2 * n_dep)),
            dma((n_col,)), dma((n_col,)), dma,
            dma((n_dep,)), dma((n_dep,)),
            dma((chunks, n_row)), dma((chunks, n_row)), dma((chunks, n_row)),
            dma((chunks, n_row)), dma((chunks, n_row)), dma((chunks, n_row)),
            dma((chunks, n_dep, 2)), dma((chunks, n_dep, 2)), dma((chunks, 2)),
        ],
        compiler_params=pltpu.CompilerParams(
            collective_id=0, has_side_effects=True, vmem_limit_bytes=60 * 1024 * 1024
        ),
        cost_estimate=pl.CostEstimate(
            flops=8 * tokens_n * depth * width,
            bytes_accessed=4 * depth * width,
            transcendentals=block * width,
        ),
    )(tokens, gate_weight, up_weight, cotangent)


def on_device(n_row, n_col, n_dep, tokens, gate_weight, up_weight, cotangent):
    depth = tokens.shape[1]
    hidden, part, all_tokens, all_gate, all_up = exchange(
        n_row, n_col, n_dep, tokens, gate_weight, up_weight, cotangent
    )
    me = lax.axis_index("col")
    rows = tokens.shape[0]
    terms = [lax.dynamic_slice_in_dim(part, me * rows, rows, 0)]
    for step in range(1, n_col):
        block = lax.dynamic_slice_in_dim(part, lax.rem(me + step, n_col) * rows, rows, 0)
        terms.append(lax.ppermute(block, "col", [(i, (i + step) % n_col) for i in range(n_col)]))
    grad_tokens = sum(term.astype(jnp.float32) for term in terms).astype(jnp.bfloat16)
    share = all_gate.shape[3]
    contract = (((0,), (0,)), ((), ()))
    flat = all_tokens.reshape(-1, depth)
    sums = [
        lax.dot_general(
            flat, grad.reshape(-1, share), contract, preferred_element_type=jnp.float32
        ).astype(jnp.bfloat16)
        for grad in (all_gate, all_up)
    ]
    return (hidden, grad_tokens, *sums)


def solution(mesh):
    sizes = tuple(mesh.shape[axis] for axis in ("row", "col", "dep"))
    return jax.shard_map(
        functools.partial(on_device, *sizes),
        mesh=mesh,
        in_specs=(
            P(("dep", "col"), "row"),
            P("row", "col"),
            P("row", "col"),
            P(("dep", "row"), "col"),
        ),
        out_specs=(
            P(("dep", "row"), "col"),
            P(("dep", "col"), "row"),
            P("row", ("col", "dep")),
            P("row", ("col", "dep")),
        ),
        check_vma=False,
    )
```

```python
import functools

import jax
import jax.numpy as jnp
from jax import lax
from jax.experimental import pallas as pl
from jax.experimental.pallas import tpu as pltpu
from jax.sharding import PartitionSpec as P

MESH = pl.DeviceIdType.MESH
WIDTH = 128
AHEAD = 2
SUM_LAG = 1
GATHER_LAG = 1
LOADED = 3


def kernel(
    n_row, n_col, n_dep, w,
    tokens_ref, gate_w_ref, up_w_ref, cot_ref,
    hidden_ref, part_ref, all_tok_ref, all_gate_ref, all_up_ref,
    tok, weights, own, from_left, from_right, grads, acc,
    w_sem, tok_send, tok_recv, tok_local, slice_send, slice_recv,
    rs_send, left_recv, right_recv, ag_right_send, ag_left_send, ag_recv,
    dep_send, dep_recv, dep_local,
):
    me = lax.axis_index("row")
    my_col = lax.axis_index("col")
    my_dep = lax.axis_index("dep")
    chunks = weights.shape[0]
    depth = weights.shape[1]
    lanes = weights.shape[2]
    share = all_gate_ref.shape[3]
    last = n_row - 1
    out_refs = (all_gate_ref, all_up_ref)
    tokens_n = tok.shape[0] * tok.shape[1]

    def weight_copy(c, h, k):
        ref = (gate_w_ref, up_w_ref)[k]
        at = pl.multiple_of(h * share + c * w, w)
        return pltpu.make_async_copy(
            ref.at[:, pl.ds(at, w)],
            weights.at[c, :, pl.ds((h * 2 + k) * w, w)],
            w_sem.at[c, h * 2 + k],
        )

    def load_weights(c):
        for h in range(n_dep):
            for k in range(2):
                weight_copy(c, h, k).start()

    barrier = pltpu.get_barrier_semaphore()
    for step in range(1, n_col):
        pl.semaphore_signal(barrier, inc=1, device_id={"col": lax.rem(my_col + step, n_col)}, device_id_type=MESH)
    for step in range(1, n_dep):
        pl.semaphore_signal(barrier, inc=1, device_id={"dep": lax.rem(my_dep + step, n_dep)}, device_id_type=MESH)

    @pl.when(me > 0)
    def _():
        pl.semaphore_signal(barrier, inc=1, device_id={"row": me - 1}, device_id_type=MESH)

    @pl.when(me < last)
    def _():
        pl.semaphore_signal(barrier, inc=1, device_id={"row": me + 1}, device_id_type=MESH)

    peers = n_col - 1 + n_dep - 1
    inside = jnp.logical_and(me > 0, me < last)

    @pl.when(inside)
    def _():
        pl.semaphore_wait(barrier, peers + 2)

    @pl.when(jnp.logical_not(inside))
    def _():
        pl.semaphore_wait(barrier, peers + 1)

    other = my_col + 1 - 2 * lax.rem(my_col, 2)

    def token_copy(step):
        return pltpu.make_async_remote_copy(
            src_ref=tokens_ref, dst_ref=tok.at[my_col],
            send_sem=tok_send.at[step], recv_sem=tok_recv.at[step],
            device_id={"col": lax.rem(my_col + step, n_col)}, device_id_type=MESH,
        )

    def pair_copy(step):
        if step == 0:
            src, at = tokens_ref, my_col
        else:
            at = lax.rem(my_col - step + n_col, n_col)
            src = tok.at[at]
        return pltpu.make_async_remote_copy(
            src_ref=src, dst_ref=tok.at[at],
            send_sem=tok_send.at[step + 1], recv_sem=tok_recv.at[step + 1],
            device_id={"col": other}, device_id_type=MESH,
        )

    for step in range(2, n_col, 2):
        token_copy(step).start()
    pair_copy(0).start()

    @pl.loop(0, LOADED)
    def _(c):
        load_weights(c)

    tok[pl.ds(my_col, 1)] = tokens_ref[...][None]
    acc[...] = jnp.zeros_like(acc)
    for step in range(2, n_col, 2):
        token_copy(step).wait_recv()
        pair_copy(step).start()
    for step in range(0, n_col, 2):
        pair_copy(step).wait_recv()

    def slice_copy(step):
        return pltpu.make_async_remote_copy(
            src_ref=tok, dst_ref=all_tok_ref.at[my_dep],
            send_sem=slice_send.at[step], recv_sem=slice_recv.at[step],
            device_id={"dep": lax.rem(my_dep + step, n_dep)}, device_id_type=MESH,
        )

    tok_out = pltpu.make_async_copy(tok, all_tok_ref.at[my_dep], tok_local)
    for step in range(1, n_dep):
        slice_copy(step).start()
    tok_out.start()

    def rs_right(c, j):
        return pltpu.make_async_remote_copy(
            src_ref=own.at[c, j], dst_ref=from_left.at[c, j],
            send_sem=rs_send.at[c, j], recv_sem=left_recv.at[c, j],
            device_id={"row": me + 1}, device_id_type=MESH,
        )

    def rs_left(c, j):
        return pltpu.make_async_remote_copy(
            src_ref=own.at[c, j], dst_ref=from_right.at[c, j],
            send_sem=rs_send.at[c, j], recv_sem=right_recv.at[c, j],
            device_id={"row": me - 1}, device_id_type=MESH,
        )

    def ag_right(c, j):
        return pltpu.make_async_remote_copy(
            src_ref=grads.at[c, j], dst_ref=grads.at[c, j],
            send_sem=ag_right_send.at[c, j], recv_sem=ag_recv.at[c, j],
            device_id={"row": me + 1}, device_id_type=MESH,
        )

    def ag_left(c, j):
        return pltpu.make_async_remote_copy(
            src_ref=grads.at[c, j], dst_ref=grads.at[c, j],
            send_sem=ag_left_send.at[c, j], recv_sem=ag_recv.at[c, j],
            device_id={"row": me - 1}, device_id_type=MESH,
        )

    def dep_copy(c, step, k):
        to = lax.rem(my_dep + step, n_dep)
        return pltpu.make_async_remote_copy(
            src_ref=grads.at[c, :, :, pl.ds(pl.multiple_of((to * 2 + k) * w, w), w)],
            dst_ref=out_refs[k].at[my_dep, :, :, pl.ds(pl.multiple_of(c * w, w), w)],
            send_sem=dep_send.at[c, step, k], recv_sem=dep_recv.at[c, step, k],
            device_id={"dep": to}, device_id_type=MESH,
        )

    def dep_own(c, k):
        return pltpu.make_async_copy(
            grads.at[c, :, :, pl.ds(pl.multiple_of((my_dep * 2 + k) * w, w), w)],
            out_refs[k].at[my_dep, :, :, pl.ds(pl.multiple_of(c * w, w), w)],
            dep_local.at[c, k],
        )

    def ready(j):
        return (jnp.maximum(j, last - j) - 1) * SUM_LAG

    def valid(c):
        return jnp.logical_and(c >= 0, c < chunks)

    def forward(c):
        for h in range(n_dep):
            for k in range(2):
                weight_copy(c, h, k).wait()
        lhs = tok[...].reshape(tokens_n, depth)
        for at in range(0, lanes, 256):
            own[c, :, :, at:at + 256] = (
                jnp.dot(lhs, weights[c, :, at:at + 256], preferred_element_type=jnp.float32)
                .astype(jnp.bfloat16)
                .reshape(n_row, tokens_n // n_row, 256)
            )

    def added(ref, other):
        ref[...] = (ref[...].astype(jnp.float32) + other[...].astype(jnp.float32)).astype(jnp.bfloat16)

    def reduce_right(c):
        for j in reversed(range(1, n_row)):
            @pl.when(j > me)
            def _():
                @pl.when(me > 0)
                def _():
                    rs_right(c, j).wait_recv()
                    added(own.at[c, j], from_left.at[c, j])
                rs_right(c, j).start()

    def reduce_left(c):
        for j in range(n_row - 1):
            @pl.when(j < me)
            def _():
                @pl.when(me < last)
                def _():
                    rs_left(c, j).wait_recv()
                    added(own.at[c, j], from_right.at[c, j])
                rs_left(c, j).start()

    def finish(c):
        @pl.when(me > 0)
        def _():
            rs_right(c, me).wait_recv()

        @pl.when(me < last)
        def _():
            rs_left(c, me).wait_recv()

        for h in range(n_dep):
            at = h * 2 * w

            def total(lo):
                piece = pl.ds(lo, w)
                value = own[c, me, :, piece].astype(jnp.float32)
                value = value + jnp.where(me > 0, from_left[c, me, :, piece].astype(jnp.float32), 0.0)
                return value + jnp.where(me < last, from_right[c, me, :, piece].astype(jnp.float32), 0.0)

            gate, up = total(at), total(at + w)
            sigma = 1.0 / (1.0 + jnp.exp(-gate))
            active = gate * sigma
            columns = pl.ds(pl.multiple_of(h * share + c * w, w), w)
            hidden_ref[:, columns] = (active * up).astype(jnp.bfloat16)
            upstream = cot_ref[:, columns].astype(jnp.float32)
            grads[c, me, :, pl.ds(at, w)] = (
                upstream * up * sigma * (1.0 + gate * (1.0 - sigma))
            ).astype(jnp.bfloat16)
            grads[c, me, :, pl.ds(at + w, w)] = (upstream * active).astype(jnp.bfloat16)

        @pl.when(me < last)
        def _():
            ag_right(c, me).start()

        @pl.when(me > 0)
        def _():
            ag_left(c, me).start()

    def relay(t):
        for away in range(1, n_row):
            c_up = t - ready(me - away) - away * GATHER_LAG
            c_down = t - ready(me + away) - away * GATHER_LAG

            @pl.when(valid(c_up))
            def _():
                c = c_up

                @pl.when(me - away >= 0)
                def _():
                    ag_right(c, me - away).wait_recv()

                    @pl.when(me < last)
                    def _():
                        ag_right(c, me - away).start()

            @pl.when(valid(c_down))
            def _():
                c = c_down

                @pl.when(me + away <= last)
                def _():
                    ag_left(c, me + away).wait_recv()

                    @pl.when(me > 0)
                    def _():
                        ag_left(c, me + away).start()

    def backward(c):
        for step in range(1, n_dep):
            for k in range(2):
                dep_copy(c, step, k).start()
        for k in range(2):
            dep_own(c, k).start()
        rhs = grads[c].reshape(tokens_n, lanes)
        tile = min(512, depth)

        @pl.loop(0, depth // tile)
        def _(i):
            rows = pl.ds(pl.multiple_of(i * tile, tile), tile)
            acc[rows] += lax.dot_general(
                weights[c, rows, :], rhs, (((1,), (1,)), ((), ())), preferred_element_type=jnp.float32
            )

    def retire(c):
        for j in range(n_row):
            @pl.when(j > me)
            def _():
                rs_right(c, j).wait_send()

            @pl.when(j < me)
            def _():
                rs_left(c, j).wait_send()

            @pl.when(jnp.logical_and(j <= me, me < last))
            def _():
                ag_right(c, j).wait_send()

            @pl.when(jnp.logical_and(j >= me, me > 0))
            def _():
                ag_left(c, j).wait_send()
        for k in range(2):
            for step in range(1, n_dep):
                dep_copy(c, step, k).wait()
            dep_own(c, k).wait()

    def start(c):
        @pl.when(c + LOADED < chunks)
        def _():
            load_weights(c + LOADED)

        forward(c)

        @pl.when(me == 0)
        def _():
            reduce_right(c)

        @pl.when(me == last)
        def _():
            reduce_left(c)

    @pl.loop(0, AHEAD)
    def _(c):
        start(c)

    length = (last - 1) * SUM_LAG + last * GATHER_LAG
    done = 0
    for j in range(n_row):
        at = (max(j, last - j) - 1) * SUM_LAG
        done = jnp.maximum(done, at + jnp.abs(me - j) * GATHER_LAG)

    @pl.loop(0, chunks + length)
    def _(t):
        @pl.when(t + AHEAD < chunks)
        def _():
            start(t + AHEAD)

        c_right = t - (me - 1) * SUM_LAG
        @pl.when(jnp.logical_and(valid(c_right), me > 0))
        def _():
            reduce_right(c_right)

        c_left = t - (last - me - 1) * SUM_LAG
        @pl.when(jnp.logical_and(valid(c_left), me < last))
        def _():
            reduce_left(c_left)

        c_own = t - ready(me)
        @pl.when(valid(c_own))
        def _():
            finish(c_own)

        relay(t)

        c_back = t - done
        @pl.when(valid(c_back))
        def _():
            backward(c_back)

        c_out = t - length - 1
        @pl.when(valid(c_out))
        def _():
            retire(c_out)

    tile = min(256, depth)
    for at in range(0, depth, tile):
        part_ref[:, at:at + tile] = acc[at:at + tile].T.astype(jnp.bfloat16)
    retire(chunks - 1)

    for step in range(2, n_col, 2):
        token_copy(step).wait_send()
    for step in range(0, n_col, 2):
        pair_copy(step).wait_send()
    for step in range(1, n_dep):
        slice_copy(step).wait()
    tok_out.wait()


def exchange(n_row, n_col, n_dep, tokens, gate_weight, up_weight, cotangent):
    rows, depth = tokens.shape
    width = gate_weight.shape[1]
    share = width // n_dep
    w = WIDTH
    chunks = share // w
    lanes = 2 * n_dep * w
    tokens_n = rows * n_col
    block = tokens_n // n_row
    bf16 = jnp.bfloat16
    vmem, hbm = pl.BlockSpec(memory_space=pltpu.VMEM), pl.BlockSpec(memory_space=pl.ANY)
    dma = pltpu.SemaphoreType.DMA
    return pl.pallas_call(
        functools.partial(kernel, n_row, n_col, n_dep, w),
        out_shape=(
            jax.ShapeDtypeStruct((block, width), bf16),
            jax.ShapeDtypeStruct((tokens_n, depth), bf16),
            jax.ShapeDtypeStruct((n_dep, n_col, rows, depth), bf16),
            jax.ShapeDtypeStruct((n_dep, n_row, block, share), bf16),
            jax.ShapeDtypeStruct((n_dep, n_row, block, share), bf16),
        ),
        in_specs=[vmem, hbm, hbm, vmem],
        out_specs=(vmem, vmem, hbm, hbm, hbm),
        scratch_shapes=[
            pltpu.VMEM((n_col, rows, depth), bf16),
            pltpu.VMEM((chunks, depth, lanes), bf16),
            pltpu.VMEM((chunks, n_row, block, lanes), bf16),
            pltpu.VMEM((chunks, n_row, block, lanes), bf16),
            pltpu.VMEM((chunks, n_row, block, lanes), bf16),
            pltpu.VMEM((chunks, n_row, block, lanes), bf16),
            pltpu.VMEM((depth, tokens_n), jnp.float32),
            dma((chunks, 2 * n_dep)),
            dma((n_col,)), dma((n_col,)), dma,
            dma((n_dep,)), dma((n_dep,)),
            dma((chunks, n_row)), dma((chunks, n_row)), dma((chunks, n_row)),
            dma((chunks, n_row)), dma((chunks, n_row)), dma((chunks, n_row)),
            dma((chunks, n_dep, 2)), dma((chunks, n_dep, 2)), dma((chunks, 2)),
        ],
        compiler_params=pltpu.CompilerParams(
            collective_id=0, has_side_effects=True, vmem_limit_bytes=60 * 1024 * 1024
        ),
        cost_estimate=pl.CostEstimate(
            flops=8 * tokens_n * depth * width,
            bytes_accessed=4 * depth * width,
            transcendentals=block * width,
        ),
    )(tokens, gate_weight, up_weight, cotangent)


def on_device(n_row, n_col, n_dep, tokens, gate_weight, up_weight, cotangent):
    depth = tokens.shape[1]
    hidden, part, all_tokens, all_gate, all_up = exchange(
        n_row, n_col, n_dep, tokens, gate_weight, up_weight, cotangent
    )
    me = lax.axis_index("col")
    rows = tokens.shape[0]
    terms = [lax.dynamic_slice_in_dim(part, me * rows, rows, 0)]
    for step in range(1, n_col):
        block = lax.dynamic_slice_in_dim(part, lax.rem(me + step, n_col) * rows, rows, 0)
        terms.append(lax.ppermute(block, "col", [(i, (i + step) % n_col) for i in range(n_col)]))
    grad_tokens = sum(term.astype(jnp.float32) for term in terms).astype(jnp.bfloat16)
    share = all_gate.shape[3]
    contract = (((0,), (0,)), ((), ()))
    flat = all_tokens.reshape(-1, depth)
    sums = [
        lax.dot_general(
            flat, grad.reshape(-1, share), contract, preferred_element_type=jnp.float32
        ).astype(jnp.bfloat16)
        for grad in (all_gate, all_up)
    ]
    return (hidden, grad_tokens, *sums)


def solution(mesh):
    sizes = tuple(mesh.shape[axis] for axis in ("row", "col", "dep"))
    return jax.shard_map(
        functools.partial(on_device, *sizes),
        mesh=mesh,
        in_specs=(
            P(("dep", "col"), "row"),
            P("row", "col"),
            P("row", "col"),
            P(("dep", "row"), "col"),
        ),
        out_specs=(
            P(("dep", "row"), "col"),
            P(("dep", "col"), "row"),
            P("row", ("col", "dep")),
            P("row", ("col", "dep")),
        ),
        check_vma=False,
    )
```

```python
import functools

import jax
import jax.numpy as jnp
from jax import lax
from jax.experimental import pallas as pl
from jax.experimental.pallas import tpu as pltpu
from jax.sharding import PartitionSpec as P

MESH = pl.DeviceIdType.MESH
WIDTH = 128
AHEAD = 2
SUM_LAG = 1
GATHER_LAG = 2
LOADED = 3


def kernel(
    n_row, n_col, n_dep, w,
    tokens_ref, gate_w_ref, up_w_ref, cot_ref,
    hidden_ref, part_ref, all_tok_ref, all_gate_ref, all_up_ref,
    tok, turned, weights, own, from_left, from_right, grads, acc,
    w_sem, tok_send, tok_recv, tok_local, slice_send, slice_recv,
    rs_send, left_recv, right_recv, ag_right_send, ag_left_send, ag_recv,
    dep_send, dep_recv, dep_local,
):
    me = lax.axis_index("row")
    my_col = lax.axis_index("col")
    my_dep = lax.axis_index("dep")
    chunks = weights.shape[0]
    depth = weights.shape[1]
    lanes = weights.shape[2]
    share = all_gate_ref.shape[3]
    last = n_row - 1
    out_refs = (all_gate_ref, all_up_ref)
    tokens_n = tok.shape[0] * tok.shape[1]

    def weight_copy(c, h, k):
        ref = (gate_w_ref, up_w_ref)[k]
        at = pl.multiple_of(h * share + c * w, w)
        return pltpu.make_async_copy(
            ref.at[:, pl.ds(at, w)],
            weights.at[c, :, pl.ds((h * 2 + k) * w, w)],
            w_sem.at[c, h * 2 + k],
        )

    def load_weights(c):
        for h in range(n_dep):
            for k in range(2):
                weight_copy(c, h, k).start()

    barrier = pltpu.get_barrier_semaphore()
    for step in range(1, n_col):
        pl.semaphore_signal(barrier, inc=1, device_id={"col": lax.rem(my_col + step, n_col)}, device_id_type=MESH)
    for step in range(1, n_dep):
        pl.semaphore_signal(barrier, inc=1, device_id={"dep": lax.rem(my_dep + step, n_dep)}, device_id_type=MESH)

    @pl.when(me > 0)
    def _():
        pl.semaphore_signal(barrier, inc=1, device_id={"row": me - 1}, device_id_type=MESH)

    @pl.when(me < last)
    def _():
        pl.semaphore_signal(barrier, inc=1, device_id={"row": me + 1}, device_id_type=MESH)

    peers = n_col - 1 + n_dep - 1
    inside = jnp.logical_and(me > 0, me < last)

    @pl.when(inside)
    def _():
        pl.semaphore_wait(barrier, peers + 2)

    @pl.when(jnp.logical_not(inside))
    def _():
        pl.semaphore_wait(barrier, peers + 1)

    other = my_col + 1 - 2 * lax.rem(my_col, 2)

    def token_copy(step):
        return pltpu.make_async_remote_copy(
            src_ref=tokens_ref, dst_ref=tok.at[my_col],
            send_sem=tok_send.at[step], recv_sem=tok_recv.at[step],
            device_id={"col": lax.rem(my_col + step, n_col)}, device_id_type=MESH,
        )

    def pair_copy(step):
        if step == 0:
            src, at = tokens_ref, my_col
        else:
            at = lax.rem(my_col - step + n_col, n_col)
            src = tok.at[at]
        return pltpu.make_async_remote_copy(
            src_ref=src, dst_ref=tok.at[at],
            send_sem=tok_send.at[step + 1], recv_sem=tok_recv.at[step + 1],
            device_id={"col": other}, device_id_type=MESH,
        )

    for step in range(2, n_col, 2):
        token_copy(step).start()
    pair_copy(0).start()

    @pl.loop(0, LOADED)
    def _(c):
        load_weights(c)

    tok[pl.ds(my_col, 1)] = tokens_ref[...][None]
    acc[...] = jnp.zeros_like(acc)
    for step in range(2, n_col, 2):
        token_copy(step).wait_recv()
        pair_copy(step).start()
    for step in range(0, n_col, 2):
        pair_copy(step).wait_recv()

    def slice_copy(step):
        return pltpu.make_async_remote_copy(
            src_ref=turned, dst_ref=all_tok_ref.at[my_dep],
            send_sem=slice_send.at[step], recv_sem=slice_recv.at[step],
            device_id={"dep": lax.rem(my_dep + step, n_dep)}, device_id_type=MESH,
        )

    tok_out = pltpu.make_async_copy(turned, all_tok_ref.at[my_dep], tok_local)

    def turn():
        tile = min(256, depth)
        for at in range(0, depth, tile):
            piece = tok[:, :, at:at + tile].reshape(tokens_n, tile)
            turned[at:at + tile] = piece.astype(jnp.float32).T.astype(jnp.bfloat16)
        for step in range(1, n_dep):
            slice_copy(step).start()
        tok_out.start()

    def rs_right(c, j):
        return pltpu.make_async_remote_copy(
            src_ref=own.at[c, j], dst_ref=from_left.at[c, j],
            send_sem=rs_send.at[c, j], recv_sem=left_recv.at[c, j],
            device_id={"row": me + 1}, device_id_type=MESH,
        )

    def rs_left(c, j):
        return pltpu.make_async_remote_copy(
            src_ref=own.at[c, j], dst_ref=from_right.at[c, j],
            send_sem=rs_send.at[c, j], recv_sem=right_recv.at[c, j],
            device_id={"row": me - 1}, device_id_type=MESH,
        )

    def ag_right(c, j):
        return pltpu.make_async_remote_copy(
            src_ref=grads.at[c, j], dst_ref=grads.at[c, j],
            send_sem=ag_right_send.at[c, j], recv_sem=ag_recv.at[c, j],
            device_id={"row": me + 1}, device_id_type=MESH,
        )

    def ag_left(c, j):
        return pltpu.make_async_remote_copy(
            src_ref=grads.at[c, j], dst_ref=grads.at[c, j],
            send_sem=ag_left_send.at[c, j], recv_sem=ag_recv.at[c, j],
            device_id={"row": me - 1}, device_id_type=MESH,
        )

    def dep_copy(c, step, k):
        to = lax.rem(my_dep + step, n_dep)
        return pltpu.make_async_remote_copy(
            src_ref=grads.at[c, :, :, pl.ds(pl.multiple_of((to * 2 + k) * w, w), w)],
            dst_ref=out_refs[k].at[my_dep, :, :, pl.ds(pl.multiple_of(c * w, w), w)],
            send_sem=dep_send.at[c, step, k], recv_sem=dep_recv.at[c, step, k],
            device_id={"dep": to}, device_id_type=MESH,
        )

    def dep_own(c, k):
        return pltpu.make_async_copy(
            grads.at[c, :, :, pl.ds(pl.multiple_of((my_dep * 2 + k) * w, w), w)],
            out_refs[k].at[my_dep, :, :, pl.ds(pl.multiple_of(c * w, w), w)],
            dep_local.at[c, k],
        )

    def ready(j):
        return (jnp.maximum(j, last - j) - 1) * SUM_LAG

    def valid(c):
        return jnp.logical_and(c >= 0, c < chunks)

    def forward(c):
        for h in range(n_dep):
            for k in range(2):
                weight_copy(c, h, k).wait()
        lhs = tok[...].reshape(tokens_n, depth)
        for at in range(0, lanes, 256):
            own[c, :, :, at:at + 256] = (
                jnp.dot(lhs, weights[c, :, at:at + 256], preferred_element_type=jnp.float32)
                .astype(jnp.bfloat16)
                .reshape(n_row, tokens_n // n_row, 256)
            )

    def added(ref, other):
        ref[...] = (ref[...].astype(jnp.float32) + other[...].astype(jnp.float32)).astype(jnp.bfloat16)

    def reduce_right(c):
        for j in reversed(range(1, n_row)):
            @pl.when(j > me)
            def _():
                @pl.when(me > 0)
                def _():
                    rs_right(c, j).wait_recv()
                    added(own.at[c, j], from_left.at[c, j])
                rs_right(c, j).start()

    def reduce_left(c):
        for j in range(n_row - 1):
            @pl.when(j < me)
            def _():
                @pl.when(me < last)
                def _():
                    rs_left(c, j).wait_recv()
                    added(own.at[c, j], from_right.at[c, j])
                rs_left(c, j).start()

    def finish(c):
        @pl.when(me > 0)
        def _():
            rs_right(c, me).wait_recv()

        @pl.when(me < last)
        def _():
            rs_left(c, me).wait_recv()

        for h in range(n_dep):
            at = h * 2 * w

            def total(lo):
                piece = pl.ds(lo, w)
                value = own[c, me, :, piece].astype(jnp.float32)
                value = value + jnp.where(me > 0, from_left[c, me, :, piece].astype(jnp.float32), 0.0)
                return value + jnp.where(me < last, from_right[c, me, :, piece].astype(jnp.float32), 0.0)

            gate, up = total(at), total(at + w)
            sigma = 1.0 / (1.0 + jnp.exp(-gate))
            active = gate * sigma
            columns = pl.ds(pl.multiple_of(h * share + c * w, w), w)
            hidden_ref[:, columns] = (active * up).astype(jnp.bfloat16)
            upstream = cot_ref[:, columns].astype(jnp.float32)
            grads[c, me, :, pl.ds(at, w)] = (
                upstream * up * sigma * (1.0 + gate * (1.0 - sigma))
            ).astype(jnp.bfloat16)
            grads[c, me, :, pl.ds(at + w, w)] = (upstream * active).astype(jnp.bfloat16)

        @pl.when(me < last)
        def _():
            ag_right(c, me).start()

        @pl.when(me > 0)
        def _():
            ag_left(c, me).start()

    def relay(t):
        for away in range(1, n_row):
            c_up = t - ready(me - away) - away * GATHER_LAG
            c_down = t - ready(me + away) - away * GATHER_LAG

            @pl.when(valid(c_up))
            def _():
                c = c_up

                @pl.when(me - away >= 0)
                def _():
                    ag_right(c, me - away).wait_recv()

                    @pl.when(me < last)
                    def _():
                        ag_right(c, me - away).start()

            @pl.when(valid(c_down))
            def _():
                c = c_down

                @pl.when(me + away <= last)
                def _():
                    ag_left(c, me + away).wait_recv()

                    @pl.when(me > 0)
                    def _():
                        ag_left(c, me + away).start()

    def backward(c):
        for step in range(1, n_dep):
            for k in range(2):
                dep_copy(c, step, k).start()
        for k in range(2):
            dep_own(c, k).start()
        rhs = grads[c].reshape(tokens_n, lanes)
        tile = min(512, depth)

        @pl.loop(0, depth // tile)
        def _(i):
            rows = pl.ds(pl.multiple_of(i * tile, tile), tile)
            acc[rows] += lax.dot_general(
                weights[c, rows, :], rhs, (((1,), (1,)), ((), ())), preferred_element_type=jnp.float32
            )

    def retire(c):
        for j in range(n_row):
            @pl.when(j > me)
            def _():
                rs_right(c, j).wait_send()

            @pl.when(j < me)
            def _():
                rs_left(c, j).wait_send()

            @pl.when(jnp.logical_and(j <= me, me < last))
            def _():
                ag_right(c, j).wait_send()

            @pl.when(jnp.logical_and(j >= me, me > 0))
            def _():
                ag_left(c, j).wait_send()
        for k in range(2):
            for step in range(1, n_dep):
                dep_copy(c, step, k).wait()
            dep_own(c, k).wait()

    def start(c):
        @pl.when(c + LOADED < chunks)
        def _():
            load_weights(c + LOADED)

        forward(c)

        @pl.when(me == 0)
        def _():
            reduce_right(c)

        @pl.when(me == last)
        def _():
            reduce_left(c)

    @pl.loop(0, AHEAD)
    def _(c):
        start(c)

    length = (last - 1) * SUM_LAG + last * GATHER_LAG
    done = 0
    for j in range(n_row):
        at = (max(j, last - j) - 1) * SUM_LAG
        done = jnp.maximum(done, at + jnp.abs(me - j) * GATHER_LAG)

    @pl.loop(0, chunks + length)
    def _(t):
        @pl.when(t + AHEAD < chunks)
        def _():
            start(t + AHEAD)

        c_right = t - (me - 1) * SUM_LAG
        @pl.when(jnp.logical_and(valid(c_right), me > 0))
        def _():
            reduce_right(c_right)

        c_left = t - (last - me - 1) * SUM_LAG
        @pl.when(jnp.logical_and(valid(c_left), me < last))
        def _():
            reduce_left(c_left)

        c_own = t - ready(me)
        @pl.when(valid(c_own))
        def _():
            finish(c_own)

        relay(t)

        @pl.when(t == 1)
        def _():
            turn()

        c_back = t - done
        @pl.when(valid(c_back))
        def _():
            backward(c_back)

        c_out = t - length - 1
        @pl.when(valid(c_out))
        def _():
            retire(c_out)

    tile = min(256, depth)
    for at in range(0, depth, tile):
        part_ref[:, at:at + tile] = acc[at:at + tile].T.astype(jnp.bfloat16)
    retire(chunks - 1)

    for step in range(2, n_col, 2):
        token_copy(step).wait_send()
    for step in range(0, n_col, 2):
        pair_copy(step).wait_send()
    for step in range(1, n_dep):
        slice_copy(step).wait()
    tok_out.wait()


def exchange(n_row, n_col, n_dep, tokens, gate_weight, up_weight, cotangent):
    rows, depth = tokens.shape
    width = gate_weight.shape[1]
    share = width // n_dep
    w = WIDTH
    chunks = share // w
    lanes = 2 * n_dep * w
    tokens_n = rows * n_col
    block = tokens_n // n_row
    bf16 = jnp.bfloat16
    vmem, hbm = pl.BlockSpec(memory_space=pltpu.VMEM), pl.BlockSpec(memory_space=pl.ANY)
    dma = pltpu.SemaphoreType.DMA
    return pl.pallas_call(
        functools.partial(kernel, n_row, n_col, n_dep, w),
        out_shape=(
            jax.ShapeDtypeStruct((block, width), bf16),
            jax.ShapeDtypeStruct((tokens_n, depth), bf16),
            jax.ShapeDtypeStruct((n_dep, depth, tokens_n), bf16),
            jax.ShapeDtypeStruct((n_dep, n_row, block, share), bf16),
            jax.ShapeDtypeStruct((n_dep, n_row, block, share), bf16),
        ),
        in_specs=[vmem, hbm, hbm, vmem],
        out_specs=(vmem, vmem, hbm, hbm, hbm),
        scratch_shapes=[
            pltpu.VMEM((n_col, rows, depth), bf16),
            pltpu.VMEM((depth, tokens_n), bf16),
            pltpu.VMEM((chunks, depth, lanes), bf16),
            pltpu.VMEM((chunks, n_row, block, lanes), bf16),
            pltpu.VMEM((chunks, n_row, block, lanes), bf16),
            pltpu.VMEM((chunks, n_row, block, lanes), bf16),
            pltpu.VMEM((chunks, n_row, block, lanes), bf16),
            pltpu.VMEM((depth, tokens_n), jnp.float32),
            dma((chunks, 2 * n_dep)),
            dma((n_col,)), dma((n_col,)), dma,
            dma((n_dep,)), dma((n_dep,)),
            dma((chunks, n_row)), dma((chunks, n_row)), dma((chunks, n_row)),
            dma((chunks, n_row)), dma((chunks, n_row)), dma((chunks, n_row)),
            dma((chunks, n_dep, 2)), dma((chunks, n_dep, 2)), dma((chunks, 2)),
        ],
        compiler_params=pltpu.CompilerParams(
            collective_id=0, has_side_effects=True, vmem_limit_bytes=60 * 1024 * 1024
        ),
        cost_estimate=pl.CostEstimate(
            flops=8 * tokens_n * depth * width,
            bytes_accessed=4 * depth * width,
            transcendentals=block * width,
        ),
    )(tokens, gate_weight, up_weight, cotangent)


def weight_grad_kernel(tokens_ref, gate_ref, up_ref, gate_out, up_out):
    n_dep, depth, _ = tokens_ref.shape
    tile = min(512, depth)
    for grad_ref, out_ref in ((gate_ref, gate_out), (up_ref, up_out)):
        for at in range(0, depth, tile):
            total = jnp.dot(tokens_ref[0, at:at + tile], grad_ref[0], preferred_element_type=jnp.float32)
            for d in range(1, n_dep):
                total = total + jnp.dot(
                    tokens_ref[d, at:at + tile], grad_ref[d], preferred_element_type=jnp.float32
                )
            out_ref[at:at + tile] = total.astype(jnp.bfloat16)


def weight_grads(turned, all_gate, all_up):
    n_dep, depth, tokens_n = turned.shape
    share = all_gate.shape[3]
    wide = 256 if share % 256 == 0 else 128
    grads = [g.reshape(n_dep, tokens_n, share) for g in (all_gate, all_up)]
    taken = pl.BlockSpec((n_dep, tokens_n, wide), lambda i: (0, 0, i))
    given = pl.BlockSpec((depth, wide), lambda i: (0, i))
    shape = jax.ShapeDtypeStruct((depth, share), jnp.bfloat16)
    return pl.pallas_call(
        weight_grad_kernel,
        grid=(share // wide,),
        in_specs=[pl.BlockSpec((n_dep, depth, tokens_n), lambda i: (0, 0, 0)), taken, taken],
        out_specs=(given, given),
        out_shape=(shape, shape),
        compiler_params=pltpu.CompilerParams(vmem_limit_bytes=48 * 1024 * 1024),
        cost_estimate=pl.CostEstimate(
            flops=4 * n_dep * tokens_n * depth * share,
            bytes_accessed=4 * depth * share + 4 * n_dep * tokens_n * share,
            transcendentals=0,
        ),
    )(turned, *grads)


def on_device(n_row, n_col, n_dep, tokens, gate_weight, up_weight, cotangent):
    depth = tokens.shape[1]
    hidden, part, all_tokens, all_gate, all_up = exchange(
        n_row, n_col, n_dep, tokens, gate_weight, up_weight, cotangent
    )
    me = lax.axis_index("col")
    rows = tokens.shape[0]
    terms = [lax.dynamic_slice_in_dim(part, me * rows, rows, 0)]
    for step in range(1, n_col):
        block = lax.dynamic_slice_in_dim(part, lax.rem(me + step, n_col) * rows, rows, 0)
        terms.append(lax.ppermute(block, "col", [(i, (i + step) % n_col) for i in range(n_col)]))
    grad_tokens = sum(term.astype(jnp.float32) for term in terms).astype(jnp.bfloat16)
    sums = weight_grads(all_tokens, all_gate, all_up)
    return (hidden, grad_tokens, *sums)


def solution(mesh):
    sizes = tuple(mesh.shape[axis] for axis in ("row", "col", "dep"))
    return jax.shard_map(
        functools.partial(on_device, *sizes),
        mesh=mesh,
        in_specs=(
            P(("dep", "col"), "row"),
            P("row", "col"),
            P("row", "col"),
            P(("dep", "row"), "col"),
        ),
        out_specs=(
            P(("dep", "row"), "col"),
            P(("dep", "col"), "row"),
            P("row", ("col", "dep")),
            P("row", ("col", "dep")),
        ),
        check_vma=False,
    )
```

```python
import functools

import jax
import jax.numpy as jnp
from jax import lax
from jax.experimental import pallas as pl
from jax.experimental.pallas import tpu as pltpu
from jax.sharding import PartitionSpec as P

MESH = pl.DeviceIdType.MESH
WIDTH = 128
AHEAD = 2
SUM_LAG = 1
GATHER_LAG = 2
LOADED = 3


def kernel(
    n_row, n_col, n_dep, w,
    tokens_ref, gate_w_ref, up_w_ref, cot_ref,
    hidden_ref, part_ref, all_tok_ref, all_gate_ref, all_up_ref,
    tok, turned, weights, own, from_left, from_right, grads, acc,
    w_sem, tok_send, tok_recv, tok_local, slice_send, slice_recv,
    rs_send, left_recv, right_recv, ag_right_send, ag_left_send, ag_recv,
    dep_send, dep_recv, dep_local,
):
    me = lax.axis_index("row")
    my_col = lax.axis_index("col")
    my_dep = lax.axis_index("dep")
    chunks = weights.shape[0]
    depth = weights.shape[1]
    lanes = weights.shape[2]
    share = all_gate_ref.shape[3]
    last = n_row - 1
    out_refs = (all_gate_ref, all_up_ref)
    tokens_n = tok.shape[0] * tok.shape[1]

    def weight_copy(c, h, k):
        ref = (gate_w_ref, up_w_ref)[k]
        at = pl.multiple_of(h * share + c * w, w)
        return pltpu.make_async_copy(
            ref.at[:, pl.ds(at, w)],
            weights.at[c, :, pl.ds((h * 2 + k) * w, w)],
            w_sem.at[c, h * 2 + k],
        )

    def load_weights(c):
        for h in range(n_dep):
            for k in range(2):
                weight_copy(c, h, k).start()

    barrier = pltpu.get_barrier_semaphore()
    for step in range(1, n_col):
        pl.semaphore_signal(barrier, inc=1, device_id={"col": lax.rem(my_col + step, n_col)}, device_id_type=MESH)
    for step in range(1, n_dep):
        pl.semaphore_signal(barrier, inc=1, device_id={"dep": lax.rem(my_dep + step, n_dep)}, device_id_type=MESH)

    @pl.when(me > 0)
    def _():
        pl.semaphore_signal(barrier, inc=1, device_id={"row": me - 1}, device_id_type=MESH)

    @pl.when(me < last)
    def _():
        pl.semaphore_signal(barrier, inc=1, device_id={"row": me + 1}, device_id_type=MESH)

    peers = n_col - 1 + n_dep - 1
    inside = jnp.logical_and(me > 0, me < last)

    @pl.when(inside)
    def _():
        pl.semaphore_wait(barrier, peers + 2)

    @pl.when(jnp.logical_not(inside))
    def _():
        pl.semaphore_wait(barrier, peers + 1)

    other = my_col + 1 - 2 * lax.rem(my_col, 2)

    def token_copy(step):
        return pltpu.make_async_remote_copy(
            src_ref=tokens_ref, dst_ref=tok.at[my_col],
            send_sem=tok_send.at[step], recv_sem=tok_recv.at[step],
            device_id={"col": lax.rem(my_col + step, n_col)}, device_id_type=MESH,
        )

    def pair_copy(step):
        if step == 0:
            src, at = tokens_ref, my_col
        else:
            at = lax.rem(my_col - step + n_col, n_col)
            src = tok.at[at]
        return pltpu.make_async_remote_copy(
            src_ref=src, dst_ref=tok.at[at],
            send_sem=tok_send.at[step + 1], recv_sem=tok_recv.at[step + 1],
            device_id={"col": other}, device_id_type=MESH,
        )

    for step in range(2, n_col, 2):
        token_copy(step).start()
    pair_copy(0).start()

    @pl.loop(0, LOADED)
    def _(c):
        load_weights(c)

    tok[pl.ds(my_col, 1)] = tokens_ref[...][None]
    acc[...] = jnp.zeros_like(acc)
    for step in range(2, n_col, 2):
        token_copy(step).wait_recv()
        pair_copy(step).start()
    for step in range(0, n_col, 2):
        pair_copy(step).wait_recv()

    def slice_copy(step):
        return pltpu.make_async_remote_copy(
            src_ref=turned, dst_ref=all_tok_ref.at[my_dep],
            send_sem=slice_send.at[step], recv_sem=slice_recv.at[step],
            device_id={"dep": lax.rem(my_dep + step, n_dep)}, device_id_type=MESH,
        )

    tok_out = pltpu.make_async_copy(turned, all_tok_ref.at[my_dep], tok_local)

    def turn():
        tile = min(256, depth)
        for at in range(0, depth, tile):
            piece = tok[:, :, at:at + tile].reshape(tokens_n, tile)
            turned[at:at + tile] = piece.astype(jnp.float32).T.astype(jnp.bfloat16)
        for step in range(1, n_dep):
            slice_copy(step).start()
        tok_out.start()

    def rs_right(c, j):
        return pltpu.make_async_remote_copy(
            src_ref=own.at[c, j], dst_ref=from_left.at[c, j],
            send_sem=rs_send.at[c, j], recv_sem=left_recv.at[c, j],
            device_id={"row": me + 1}, device_id_type=MESH,
        )

    def rs_left(c, j):
        return pltpu.make_async_remote_copy(
            src_ref=own.at[c, j], dst_ref=from_right.at[c, j],
            send_sem=rs_send.at[c, j], recv_sem=right_recv.at[c, j],
            device_id={"row": me - 1}, device_id_type=MESH,
        )

    def ag_right(c, j):
        return pltpu.make_async_remote_copy(
            src_ref=grads.at[c, j], dst_ref=grads.at[c, j],
            send_sem=ag_right_send.at[c, j], recv_sem=ag_recv.at[c, j],
            device_id={"row": me + 1}, device_id_type=MESH,
        )

    def ag_left(c, j):
        return pltpu.make_async_remote_copy(
            src_ref=grads.at[c, j], dst_ref=grads.at[c, j],
            send_sem=ag_left_send.at[c, j], recv_sem=ag_recv.at[c, j],
            device_id={"row": me - 1}, device_id_type=MESH,
        )

    def dep_copy(c, step, k):
        to = lax.rem(my_dep + step, n_dep)
        return pltpu.make_async_remote_copy(
            src_ref=grads.at[c, :, :, pl.ds(pl.multiple_of((to * 2 + k) * w, w), w)],
            dst_ref=out_refs[k].at[my_dep, :, :, pl.ds(pl.multiple_of(c * w, w), w)],
            send_sem=dep_send.at[c, step, k], recv_sem=dep_recv.at[c, step, k],
            device_id={"dep": to}, device_id_type=MESH,
        )

    def dep_own(c, k):
        return pltpu.make_async_copy(
            grads.at[c, :, :, pl.ds(pl.multiple_of((my_dep * 2 + k) * w, w), w)],
            out_refs[k].at[my_dep, :, :, pl.ds(pl.multiple_of(c * w, w), w)],
            dep_local.at[c, k],
        )

    def ready(j):
        return (jnp.maximum(j, last - j) - 1) * SUM_LAG

    def valid(c):
        return jnp.logical_and(c >= 0, c < chunks)

    def forward(c):
        for h in range(n_dep):
            for k in range(2):
                weight_copy(c, h, k).wait()
        lhs = tok[...].reshape(tokens_n, depth)
        for at in range(0, lanes, 256):
            own[c, :, :, at:at + 256] = (
                jnp.dot(lhs, weights[c, :, at:at + 256], preferred_element_type=jnp.float32)
                .astype(jnp.bfloat16)
                .reshape(n_row, tokens_n // n_row, 256)
            )

    def added(ref, other):
        ref[...] = (ref[...].astype(jnp.float32) + other[...].astype(jnp.float32)).astype(jnp.bfloat16)

    def reduce_right(c):
        for j in reversed(range(1, n_row)):
            @pl.when(j > me)
            def _():
                @pl.when(me > 0)
                def _():
                    rs_right(c, j).wait_recv()
                    added(own.at[c, j], from_left.at[c, j])
                rs_right(c, j).start()

    def reduce_left(c):
        for j in range(n_row - 1):
            @pl.when(j < me)
            def _():
                @pl.when(me < last)
                def _():
                    rs_left(c, j).wait_recv()
                    added(own.at[c, j], from_right.at[c, j])
                rs_left(c, j).start()

    def finish(c):
        @pl.when(me > 0)
        def _():
            rs_right(c, me).wait_recv()

        @pl.when(me < last)
        def _():
            rs_left(c, me).wait_recv()

        for h in range(n_dep):
            at = h * 2 * w

            def total(lo):
                piece = pl.ds(lo, w)
                value = own[c, me, :, piece].astype(jnp.float32)
                value = value + jnp.where(me > 0, from_left[c, me, :, piece].astype(jnp.float32), 0.0)
                return value + jnp.where(me < last, from_right[c, me, :, piece].astype(jnp.float32), 0.0)

            gate, up = total(at), total(at + w)
            sigma = 1.0 / (1.0 + jnp.exp(-gate))
            active = gate * sigma
            columns = pl.ds(pl.multiple_of(h * share + c * w, w), w)
            hidden_ref[:, columns] = (active * up).astype(jnp.bfloat16)
            upstream = cot_ref[:, columns].astype(jnp.float32)
            grads[c, me, :, pl.ds(at, w)] = (
                upstream * up * sigma * (1.0 + gate * (1.0 - sigma))
            ).astype(jnp.bfloat16)
            grads[c, me, :, pl.ds(at + w, w)] = (upstream * active).astype(jnp.bfloat16)

        @pl.when(me < last)
        def _():
            ag_right(c, me).start()

        @pl.when(me > 0)
        def _():
            ag_left(c, me).start()

    def relay(t):
        for away in range(1, n_row):
            c_up = t - ready(me - away) - away * GATHER_LAG
            c_down = t - ready(me + away) - away * GATHER_LAG

            @pl.when(valid(c_up))
            def _():
                c = c_up

                @pl.when(me - away >= 0)
                def _():
                    ag_right(c, me - away).wait_recv()

                    @pl.when(me < last)
                    def _():
                        ag_right(c, me - away).start()

            @pl.when(valid(c_down))
            def _():
                c = c_down

                @pl.when(me + away <= last)
                def _():
                    ag_left(c, me + away).wait_recv()

                    @pl.when(me > 0)
                    def _():
                        ag_left(c, me + away).start()

    def backward(c):
        for step in range(1, n_dep):
            for k in range(2):
                dep_copy(c, step, k).start()
        for k in range(2):
            dep_own(c, k).start()
        rhs = grads[c].reshape(tokens_n, lanes)
        tile = min(512, depth)

        @pl.loop(0, depth // tile)
        def _(i):
            rows = pl.ds(pl.multiple_of(i * tile, tile), tile)
            acc[rows] += lax.dot_general(
                weights[c, rows, :], rhs, (((1,), (1,)), ((), ())), preferred_element_type=jnp.float32
            )

    def retire(c):
        for j in range(n_row):
            @pl.when(j > me)
            def _():
                rs_right(c, j).wait_send()

            @pl.when(j < me)
            def _():
                rs_left(c, j).wait_send()

            @pl.when(jnp.logical_and(j <= me, me < last))
            def _():
                ag_right(c, j).wait_send()

            @pl.when(jnp.logical_and(j >= me, me > 0))
            def _():
                ag_left(c, j).wait_send()
        for k in range(2):
            for step in range(1, n_dep):
                dep_copy(c, step, k).wait()
            dep_own(c, k).wait()

    def start(c):
        @pl.when(c + LOADED < chunks)
        def _():
            load_weights(c + LOADED)

        forward(c)

        @pl.when(me == 0)
        def _():
            reduce_right(c)

        @pl.when(me == last)
        def _():
            reduce_left(c)

    @pl.loop(0, AHEAD)
    def _(c):
        start(c)

    length = (last - 1) * SUM_LAG + last * GATHER_LAG
    done = 0
    for j in range(n_row):
        at = (max(j, last - j) - 1) * SUM_LAG
        done = jnp.maximum(done, at + jnp.abs(me - j) * GATHER_LAG)

    @pl.loop(0, chunks + length)
    def _(t):
        @pl.when(t + AHEAD < chunks)
        def _():
            start(t + AHEAD)

        c_right = t - (me - 1) * SUM_LAG
        @pl.when(jnp.logical_and(valid(c_right), me > 0))
        def _():
            reduce_right(c_right)

        c_left = t - (last - me - 1) * SUM_LAG
        @pl.when(jnp.logical_and(valid(c_left), me < last))
        def _():
            reduce_left(c_left)

        c_own = t - ready(me)
        @pl.when(valid(c_own))
        def _():
            finish(c_own)

        relay(t)

        @pl.when(t == 1)
        def _():
            turn()

        c_back = t - done
        @pl.when(valid(c_back))
        def _():
            backward(c_back)

        c_out = t - length - 1
        @pl.when(valid(c_out))
        def _():
            retire(c_out)

    tile = min(256, depth)
    for at in range(0, depth, tile):
        part_ref[:, at:at + tile] = acc[at:at + tile].T.astype(jnp.bfloat16)
    retire(chunks - 1)

    for step in range(2, n_col, 2):
        token_copy(step).wait_send()
    for step in range(0, n_col, 2):
        pair_copy(step).wait_send()
    for step in range(1, n_dep):
        slice_copy(step).wait()
    tok_out.wait()


def exchange(n_row, n_col, n_dep, tokens, gate_weight, up_weight, cotangent):
    rows, depth = tokens.shape
    width = gate_weight.shape[1]
    share = width // n_dep
    w = WIDTH
    chunks = share // w
    lanes = 2 * n_dep * w
    tokens_n = rows * n_col
    block = tokens_n // n_row
    bf16 = jnp.bfloat16
    vmem, hbm = pl.BlockSpec(memory_space=pltpu.VMEM), pl.BlockSpec(memory_space=pl.ANY)
    dma = pltpu.SemaphoreType.DMA
    return pl.pallas_call(
        functools.partial(kernel, n_row, n_col, n_dep, w),
        out_shape=(
            jax.ShapeDtypeStruct((block, width), bf16),
            jax.ShapeDtypeStruct((tokens_n, depth), bf16),
            jax.ShapeDtypeStruct((n_dep, depth, tokens_n), bf16),
            jax.ShapeDtypeStruct((n_dep, n_row, block, share), bf16),
            jax.ShapeDtypeStruct((n_dep, n_row, block, share), bf16),
        ),
        in_specs=[vmem, hbm, hbm, vmem],
        out_specs=(vmem, vmem, hbm, hbm, hbm),
        scratch_shapes=[
            pltpu.VMEM((n_col, rows, depth), bf16),
            pltpu.VMEM((depth, tokens_n), bf16),
            pltpu.VMEM((chunks, depth, lanes), bf16),
            pltpu.VMEM((chunks, n_row, block, lanes), bf16),
            pltpu.VMEM((chunks, n_row, block, lanes), bf16),
            pltpu.VMEM((chunks, n_row, block, lanes), bf16),
            pltpu.VMEM((chunks, n_row, block, lanes), bf16),
            pltpu.VMEM((depth, tokens_n), jnp.float32),
            dma((chunks, 2 * n_dep)),
            dma((n_col,)), dma((n_col,)), dma,
            dma((n_dep,)), dma((n_dep,)),
            dma((chunks, n_row)), dma((chunks, n_row)), dma((chunks, n_row)),
            dma((chunks, n_row)), dma((chunks, n_row)), dma((chunks, n_row)),
            dma((chunks, n_dep, 2)), dma((chunks, n_dep, 2)), dma((chunks, 2)),
        ],
        compiler_params=pltpu.CompilerParams(
            collective_id=0, has_side_effects=True, vmem_limit_bytes=60 * 1024 * 1024
        ),
        cost_estimate=pl.CostEstimate(
            flops=8 * tokens_n * depth * width,
            bytes_accessed=4 * depth * width,
            transcendentals=block * width,
        ),
    )(tokens, gate_weight, up_weight, cotangent)


def weight_grad_kernel(tokens_ref, gate_ref, up_ref, gate_out, up_out):
    n_dep, depth, _ = tokens_ref.shape
    tile = min(512, depth)
    for grad_ref, out_ref in ((gate_ref, gate_out), (up_ref, up_out)):
        for at in range(0, depth, tile):
            total = jnp.dot(tokens_ref[0, at:at + tile], grad_ref[0], preferred_element_type=jnp.float32)
            for d in range(1, n_dep):
                total = total + jnp.dot(
                    tokens_ref[d, at:at + tile], grad_ref[d], preferred_element_type=jnp.float32
                )
            out_ref[at:at + tile] = total.astype(jnp.bfloat16)


def weight_grads(turned, all_gate, all_up):
    n_dep, depth, tokens_n = turned.shape
    share = all_gate.shape[3]
    wide = 256 if share % 256 == 0 else 128
    grads = [g.reshape(n_dep, tokens_n, share) for g in (all_gate, all_up)]
    taken = pl.BlockSpec((n_dep, tokens_n, wide), lambda i: (0, 0, i))
    given = pl.BlockSpec((depth, wide), lambda i: (0, i))
    shape = jax.ShapeDtypeStruct((depth, share), jnp.bfloat16)
    return pl.pallas_call(
        weight_grad_kernel,
        grid=(share // wide,),
        in_specs=[pl.BlockSpec((n_dep, depth, tokens_n), lambda i: (0, 0, 0)), taken, taken],
        out_specs=(given, given),
        out_shape=(shape, shape),
        compiler_params=pltpu.CompilerParams(vmem_limit_bytes=60 * 1024 * 1024),
        cost_estimate=pl.CostEstimate(
            flops=4 * n_dep * tokens_n * depth * share,
            bytes_accessed=4 * depth * share + 4 * n_dep * tokens_n * share,
            transcendentals=0,
        ),
    )(turned, *grads)


def on_device(n_row, n_col, n_dep, tokens, gate_weight, up_weight, cotangent):
    depth = tokens.shape[1]
    hidden, part, all_tokens, all_gate, all_up = exchange(
        n_row, n_col, n_dep, tokens, gate_weight, up_weight, cotangent
    )
    me = lax.axis_index("col")
    rows = tokens.shape[0]
    terms = [lax.dynamic_slice_in_dim(part, me * rows, rows, 0)]
    for step in range(1, n_col):
        block = lax.dynamic_slice_in_dim(part, lax.rem(me + step, n_col) * rows, rows, 0)
        terms.append(lax.ppermute(block, "col", [(i, (i + step) % n_col) for i in range(n_col)]))
    grad_tokens = sum(term.astype(jnp.float32) for term in terms).astype(jnp.bfloat16)
    sums = weight_grads(all_tokens, all_gate, all_up)
    return (hidden, grad_tokens, *sums)


def solution(mesh):
    sizes = tuple(mesh.shape[axis] for axis in ("row", "col", "dep"))
    return jax.shard_map(
        functools.partial(on_device, *sizes),
        mesh=mesh,
        in_specs=(
            P(("dep", "col"), "row"),
            P("row", "col"),
            P("row", "col"),
            P(("dep", "row"), "col"),
        ),
        out_specs=(
            P(("dep", "row"), "col"),
            P(("dep", "col"), "row"),
            P("row", ("col", "dep")),
            P("row", ("col", "dep")),
        ),
        check_vma=False,
    )
```
